32 devices in a mesh: groups: 2 (over x), dates: 16 (over z, y, core).
Axes of the slice: x: 2, y: 2, z: 4, core: 2. Of those that a mesh axis runs over, the one named last changes fastest.
Arguments:
- scenes: bfloat16 [64, 16, 7, 256], P(('groups', 'dates')), parts along dimension 0, as said below
- quality: bfloat16 [64, 16, 256], P(('groups', 'dates')), parts along dimension 0, may hold values from 0.099609375 to 1
- pif_mask: float32 [32, 256], P(('groups', 'dates')), parts along dimension 0, may hold values from 0.05 to 1
- counts: int32 [32], P(('groups', 'dates')), parts along dimension 0, may hold values from 1 to 32, as said below
Outputs:
- normalized: bfloat16 [64, 16, 7, 256], P(('groups', 'dates')), parts along dimension 0
The draws below stay inside these ranges and needn't reach their ends.
There are 2 independent parts, one for each index of `groups`. The reference program is written for one: setup_inputs(seed, part) draws one part's arguments, and reference() takes and returns one part's arrays. A program takes and returns all parts, laid end to end along the dimension named above; each array names one. Nothing has to cross between parts.
Inputs may be any that keep to these rules, and one draw needn't show every extreme that they name: Tile t is valid on dates 0 to counts[t] - 1; some tile is valid on all 32 dates. scenes are finite reflectances.
All inputs are finite; a program needn't handle non-finite values.
Results may differ from the reference program's by a relative error of at most 0.0005.
Values may be sent and summed in bfloat16 or wider, within the bound.
No kernel may reach another device: no remote copies, remote signals or barrier semaphores. Data moves between devices by JAX's collectives and lax.ppermute only.
A program may use at most 64 MiB of HBM per device.

```python
import math
import jax
import jax.numpy as jnp
from jax import lax

BANDS = 7
PIX = 256
DATES = 32
TILES = 16


def draw_scenes(key, part):
    keys = jax.random.split(jax.random.fold_in(key, 11), 4)
    surface = jax.random.normal(keys[0], (TILES, BANDS, PIX), jnp.float32)
    date_gain = jax.random.uniform(keys[1], (DATES, BANDS), jnp.float32, 0.6, 1.6)
    date_shift = 0.5 * jax.random.normal(keys[2], (DATES, BANDS), jnp.float32)
    noise = 0.3 * jax.random.normal(keys[3], (DATES, TILES, BANDS, PIX), jnp.float32)
    values = surface[None] * date_gain[:, None, :, None] + date_shift[:, None, :, None] + noise
    return values.astype(jnp.bfloat16)


def draw_counts(key, part):
    keys = jax.random.split(jax.random.fold_in(key, 23), 3)
    first = jax.random.randint(keys[0], (TILES,), 0, DATES)
    second = jax.random.randint(keys[1], (TILES,), 0, DATES)
    valid = 1 + first * second // DATES
    where = jax.random.randint(keys[2], (), 0, TILES)
    return valid.at[where].set(DATES).astype(jnp.int32)


def steps_of(stream_key, dims, shards, smallest, largest):
    def one(axis_at, blocks):
        heights = jax.random.uniform(jax.random.fold_in(jax.random.fold_in(stream_key, 6), axis_at), (blocks,), jnp.float32, smallest / len(shards), largest / len(shards))
        return jnp.repeat(jnp.exp(heights), dims[axis_at] // blocks).reshape((-1,) + (1,) * (len(dims) - axis_at - 1))

    level = one(*shards[0])
    for cut in shards[1:]:
        level = level * one(*cut)
    return level


def setup_inputs(seed: int = 0, part: int = 0) -> dict:
    arg_keys = jax.random.split(jax.random.key(seed), 5)
    part_keys = jax.random.split(jax.random.fold_in(arg_keys[4], part), 5)
    return {
        "scenes": draw_scenes(jax.random.fold_in(jax.random.fold_in(arg_keys[4], part), 71), part),
        "quality": jnp.clip(0.099609375 + 0.9003906 * jax.random.uniform(part_keys[1], (DATES, TILES, PIX), jnp.float32) ** steps_of(part_keys[1], (DATES, TILES, PIX), ((0, 16),), -0.2, 0.2), 0.099609375, 1.0).astype(jnp.bfloat16),
        "pif_mask": jnp.clip(jnp.exp(math.log(1.0) - 2.9957323 * jax.random.uniform(part_keys[2], (TILES, PIX), jnp.float32) ** steps_of(part_keys[2], (TILES, PIX), ((0, 16),), -0.2, 0.2)), 0.05, 1.0),
        "counts": draw_counts(jax.random.fold_in(jax.random.fold_in(arg_keys[4], part), 71), part),
    }


def solve_fit(weight_sum, sum_x, sum_xx, sum_y, sum_xy):
    total = weight_sum[:, None]
    mean_x = sum_x / total
    mean_y = sum_y / total
    spread = sum_xx / total - mean_x * mean_x + 1e-5
    gain = (sum_xy / total - mean_x * mean_y) / spread
    return gain, mean_y - gain * mean_x


def reference(scenes, quality, pif_mask, counts):
    date_ids = jnp.arange(DATES, dtype=jnp.int32)
    covered = (date_ids[:, None] < counts[None, :]).astype(jnp.float32)

    def accumulate(carry, item):
        weighted, totals = carry
        scene, qual, cover = item
        weight = qual.astype(jnp.float32) * cover[:, None]
        return (weighted + weight[:, None, :] * scene.astype(jnp.float32), totals + weight), None

    start = (jnp.zeros((TILES, BANDS, PIX), jnp.float32), jnp.zeros((TILES, PIX), jnp.float32))
    (weighted, totals), _ = lax.scan(accumulate, start, (scenes, quality, covered))
    composite = weighted / totals[:, None, :]

    def partials(item):
        scene, qual, cover = item
        fit = qual.astype(jnp.float32) * cover[:, None] * pif_mask
        values = scene.astype(jnp.float32)
        fitted = fit[:, None, :] * values
        return (jnp.sum(fit), jnp.sum(fitted, axis=(0, 2)), jnp.sum(fitted * values, axis=(0, 2)),
                jnp.sum(fit[:, None, :] * composite, axis=(0, 2)), jnp.sum(fitted * composite, axis=(0, 2)))

    weight_sum, sum_x, sum_xx, sum_y, sum_xy = lax.map(partials, (scenes, quality, covered))
    gain, offset = solve_fit(weight_sum, sum_x, sum_xx, sum_y, sum_xy)

    def apply_fit(item):
        scene, slope, shift = item
        return (slope[None, :, None] * scene.astype(jnp.float32) + shift[None, :, None]).astype(jnp.bfloat16)

    return lax.map(apply_fit, (scenes, gain, offset))
```

```python
import functools
import jax
import jax.numpy as jnp
from jax import lax
from jax.experimental import pallas as pl
from jax.experimental.pallas import tpu as pltpu
from jax.sharding import PartitionSpec as P

F32 = jnp.float32
LANES = 128
VMEM = pl.BlockSpec(memory_space=pltpu.VMEM)
SMEM = pl.BlockSpec(memory_space=pltpu.SMEM)


def near(x):
    return pltpu.with_memory_space_constraint(x, pltpu.VMEM)


def tile_kernel(size, pif_ref, counts_ref, out_ref):
    half, width = out_ref.shape
    pixels = pif_ref.shape[-1]
    me = lax.axis_index("dates")
    row = lax.broadcasted_iota(jnp.int32, (half, width), 0)
    count = jnp.full((half, LANES), counts_ref[0], jnp.int32).astype(F32)
    pif = jnp.broadcast_to(pif_ref[...], (half, pixels))
    tile = jnp.concatenate([pif, count], axis=1)
    out_ref[...] = jnp.where(row == me % (size // 2), tile, 0.0)


def split_kernel(size, scenes_ref, quality_ref, keep_ref, send_ref, copy_ref):
    dates, bands, tiles, _ = scenes_ref.shape
    half = tiles // 2
    low = lax.axis_index("dates") < size // 2
    for d in range(dates):
        for b in range(bands + 1):
            whole = scenes_ref[d, b] if b < bands else quality_ref[d]
            if b < bands:
                copy_ref[d, b] = whole
            whole = whole.astype(F32)
            lower, upper = whole[:half], whole[half:]
            keep_ref[d, b] = jnp.where(low, lower, upper).astype(keep_ref.dtype)
            send_ref[d, b] = jnp.where(low, upper, lower).astype(send_ref.dtype)


def weight_of(quality, date, count):
    covered = (count > date.astype(F32)).astype(F32)
    return quality.astype(F32) * jnp.concatenate(
        [covered] * (quality.shape[-1] // LANES), axis=1
    )


def first_dates(size, dates):
    me = lax.axis_index("dates")
    return me * dates, (me ^ (size // 2)) * dates


def partial_kernel(size, keep_ref, got_ref, tile_ref, out_ref):
    dates, rows, half, pixels = keep_ref.shape
    count = tile_ref[:, pixels:]
    weights = [
        (ref, d, weight_of(ref[d, rows - 1], first + d, count))
        for first, ref in zip(first_dates(size, dates), (keep_ref, got_ref))
        for d in range(dates)
    ]
    for b in range(rows - 1):
        out_ref[b] = sum(w * ref[d, b].astype(F32) for ref, d, w in weights)
    out_ref[rows - 1] = sum(w for _, _, w in weights)


def fold(term):
    pixels = term.shape[-1]
    term = sum(term[:, p : p + LANES] for p in range(0, pixels, LANES))
    return jnp.sum(term, axis=0, keepdims=True)


def fit_kernel(size, keep_ref, got_ref, tile_ref, *refs):
    *part_refs, own_ref, other_ref = refs
    dates, rows, half, pixels = keep_ref.shape
    count, pif = tile_ref[:, pixels:], tile_ref[:, :pixels]
    total = [sum(ref[b] for ref in part_refs) for b in range(rows)]
    composite = [total[b] / total[rows - 1] for b in range(rows - 1)]
    sides = zip(first_dates(size, dates), (keep_ref, got_ref), (own_ref, other_ref))
    for first, ref, out in sides:
        for d in range(dates):
            fit = weight_of(ref[d, rows - 1], first + d, count) * pif
            sums = ([], [], [], [])
            for b in range(rows - 1):
                x, y = ref[d, b].astype(F32), composite[b]
                fitted = fit * x
                for kind, term in zip(sums, (fitted, fitted * x, fit * y, fitted * y)):
                    kind.append(fold(term))
            weight = fold(fit)
            for k, kind in enumerate(sums):
                out[d, k] = jnp.concatenate(kind + [weight], axis=0)


def apply_kernel(own_ref, got_ref, scenes_ref, out_ref):
    dates, bands, tiles, pixels = scenes_ref.shape
    sums = own_ref[...] + got_ref[...]
    sums = jnp.sum(sums, axis=-1, keepdims=True)
    for d in range(dates):
        sum_x, sum_xx, sum_y, sum_xy = (sums[d, k, :bands] for k in range(4))
        total = sums[d, 0, bands : bands + 1]
        mean_x = sum_x / total
        mean_y = sum_y / total
        spread = sum_xx / total - mean_x * mean_x + 1e-05
        gain = (sum_xy / total - mean_x * mean_y) / spread
        offset = mean_y - gain * mean_x
        for b in range(bands):
            values = scenes_ref[d, b].astype(F32)
            out_ref[d, b] = (gain[b : b + 1] * values + offset[b : b + 1]).astype(
                out_ref.dtype
            )


def local(size, scenes, quality, pif_mask, counts):
    dates, tiles, bands, pixels = scenes.shape
    scenes = scenes.transpose(0, 2, 1, 3)
    rows, half = bands + 1, tiles // 2
    top = size // 2

    def swap(x, k):
        return lax.ppermute(x, "dates", [(i, i ^ k) for i in range(size)])

    def add_up(x, keep_last=False):
        bit, groups = 1, []
        while bit < top:
            wide = bit > 1 and bit * 2 < top
            groups.append([3 * bit, 2 * bit, bit] if wide else [bit])
            bit *= 4 if wide else 2
        for group in groups[: -1 if keep_last else None]:
            x = sum([swap(x, k) for k in group[::-1]], x)
        if keep_last:
            return [x] + [swap(x, k) for k in groups[-1][::-1]]
        return x

    tile = pl.pallas_call(
        functools.partial(tile_kernel, size),
        out_shape=pltpu.VMEM((half, pixels + LANES), F32),
        in_specs=[VMEM, SMEM],
        out_specs=VMEM,
    )(pif_mask, counts)
    tile = near(add_up(tile))
    shape = (dates, rows, half, pixels)
    keep, send, copy = pl.pallas_call(
        functools.partial(split_kernel, size),
        out_shape=[
            pltpu.VMEM(shape, scenes.dtype),
            pltpu.VMEM(shape, scenes.dtype),
            pltpu.VMEM(scenes.shape, scenes.dtype),
        ],
        in_specs=[VMEM, VMEM],
        out_specs=[VMEM] * 3,
    )(scenes, quality)
    got = near(swap(send, top))
    keep, copy = near(keep), near(copy)
    part = pl.pallas_call(
        functools.partial(partial_kernel, size),
        out_shape=pltpu.VMEM(shape[1:], F32),
        in_specs=[VMEM] * 3,
        out_specs=VMEM,
    )(keep, got, tile)
    parts = add_up(part, keep_last=True)
    sums = pltpu.VMEM((dates, 4, rows, LANES), F32)
    own, other = pl.pallas_call(
        functools.partial(fit_kernel, size),
        out_shape=[sums, sums],
        in_specs=[VMEM] * (3 + len(parts)),
        out_specs=[VMEM] * 2,
    )(keep, got, tile, *map(near, parts))
    out = pl.pallas_call(
        apply_kernel,
        out_shape=jax.ShapeDtypeStruct(scenes.shape, scenes.dtype),
        in_specs=[VMEM] * 3,
        out_specs=VMEM,
    )(near(own), near(swap(other, top)), copy)
    return out.transpose(0, 2, 1, 3)


def solution(mesh):
    placed = (
        P(("groups", "dates"), None, None, None),
        P(("groups", "dates"), None, None),
        P(("groups", "dates"), None),
        P(("groups", "dates")),
    )
    return jax.shard_map(
        functools.partial(local, mesh.shape["dates"]),
        mesh=mesh,
        in_specs=placed,
        out_specs=P(("groups", "dates"), None, None, None),
        check_vma=False,
    )
```

```python
import functools
import jax
import jax.numpy as jnp
from jax import lax
from jax.experimental import pallas as pl
from jax.experimental.pallas import tpu as pltpu
from jax.sharding import PartitionSpec as P

F32 = jnp.float32
LANES = 128
VMEM = pl.BlockSpec(memory_space=pltpu.VMEM)
SMEM = pl.BlockSpec(memory_space=pltpu.SMEM)


def near(x):
    return pltpu.with_memory_space_constraint(x, pltpu.VMEM)


def split_kernel(
    size, scenes_ref, quality_ref, pif_ref, counts_ref, tile_ref, keep_ref, send_ref, copy_ref
):
    dates, bands, tiles, pixels = scenes_ref.shape
    half = tiles // 2
    me = lax.axis_index("dates")
    row = lax.broadcasted_iota(jnp.int32, tile_ref.shape, 0)
    count = jnp.broadcast_to(counts_ref[...].astype(F32), (half, LANES))
    pif = jnp.broadcast_to(pif_ref[...], (half, pixels))
    tile = jnp.concatenate([pif, count], axis=1)
    tile_ref[...] = jnp.where(row == me % (size // 2), tile, 0.0)
    low = me < size // 2
    for d in range(dates):
        for b in range(bands + 1):
            whole = scenes_ref[d, b] if b < bands else quality_ref[d]
            if b < bands:
                copy_ref[d, b] = whole
            whole = whole.astype(F32)
            lower, upper = whole[:half], whole[half:]
            keep_ref[d, b] = jnp.where(low, lower, upper).astype(keep_ref.dtype)
            send_ref[d, b] = jnp.where(low, upper, lower).astype(send_ref.dtype)


def weight_of(quality, date, count):
    covered = (count > date.astype(F32)).astype(F32)
    return quality.astype(F32) * jnp.concatenate(
        [covered] * (quality.shape[-1] // LANES), axis=1
    )


def first_dates(size, dates):
    me = lax.axis_index("dates")
    return me * dates, (me ^ (size // 2)) * dates


def partial_kernel(size, keep_ref, got_ref, tile_ref, out_ref):
    dates, rows, half, pixels = keep_ref.shape
    count = tile_ref[:, pixels:]
    weights = [
        (ref, d, weight_of(ref[d, rows - 1], first + d, count))
        for first, ref in zip(first_dates(size, dates), (keep_ref, got_ref))
        for d in range(dates)
    ]
    for b in range(rows - 1):
        out_ref[b] = sum(w * ref[d, b].astype(F32) for ref, d, w in weights)
    out_ref[rows - 1] = sum(w for _, _, w in weights)


def fold(term):
    pixels = term.shape[-1]
    term = sum(term[:, p : p + LANES] for p in range(0, pixels, LANES))
    return jnp.sum(term, axis=0, keepdims=True)


def fit_kernel(size, keep_ref, got_ref, tile_ref, *refs):
    *part_refs, own_ref, other_ref = refs
    dates, rows, half, pixels = keep_ref.shape
    count, pif = tile_ref[:, pixels:], tile_ref[:, :pixels]
    total = [sum(ref[b] for ref in part_refs) for b in range(rows)]
    composite = [total[b] / total[rows - 1] for b in range(rows - 1)]
    sides = zip(first_dates(size, dates), (keep_ref, got_ref), (own_ref, other_ref))
    for first, ref, out in sides:
        for d in range(dates):
            fit = weight_of(ref[d, rows - 1], first + d, count) * pif
            sums = ([], [], [], [])
            for b in range(rows - 1):
                x, y = ref[d, b].astype(F32), composite[b]
                fitted = fit * x
                for kind, term in zip(sums, (fitted, fitted * x, fit * y, fitted * y)):
                    kind.append(fold(term))
            weight = fold(fit)
            for k, kind in enumerate(sums):
                out[d, k] = jnp.concatenate(kind + [weight], axis=0)


def apply_kernel(own_ref, got_ref, scenes_ref, out_ref):
    dates, bands, tiles, pixels = scenes_ref.shape
    sums = own_ref[...] + got_ref[...]
    sums = jnp.sum(sums, axis=-1, keepdims=True)
    for d in range(dates):
        sum_x, sum_xx, sum_y, sum_xy = (sums[d, k, :bands] for k in range(4))
        total = sums[d, 0, bands : bands + 1]
        mean_x = sum_x / total
        mean_y = sum_y / total
        spread = sum_xx / total - mean_x * mean_x + 1e-05
        gain = (sum_xy / total - mean_x * mean_y) / spread
        offset = mean_y - gain * mean_x
        for b in range(bands):
            values = scenes_ref[d, b].astype(F32)
            out_ref[d, b] = (gain[b : b + 1] * values + offset[b : b + 1]).astype(
                out_ref.dtype
            )


def local(size, scenes, quality, pif_mask, counts):
    dates, tiles, bands, pixels = scenes.shape
    scenes = scenes.transpose(0, 2, 1, 3)
    rows, half = bands + 1, tiles // 2
    top = size // 2

    def swap(x, k):
        return lax.ppermute(x, "dates", [(i, i ^ k) for i in range(size)])

    bit, groups = 2, []
    while bit < top:
        wide = bit * 2 < top
        groups.append([3 * bit, 2 * bit, bit] if wide else [bit])
        bit *= 4 if wide else 2

    def parts_of(x, group):
        return [x] + [swap(x, k) for k in group[::-1]]

    shape = (dates, rows, half, pixels)
    tile, keep, send, copy = pl.pallas_call(
        functools.partial(split_kernel, size),
        out_shape=[
            pltpu.VMEM((half, pixels + LANES), F32),
            pltpu.VMEM(shape, scenes.dtype),
            pltpu.VMEM(shape, scenes.dtype),
            pltpu.VMEM(scenes.shape, scenes.dtype),
        ],
        in_specs=[VMEM] * 4,
        out_specs=[VMEM] * 4,
    )(scenes, quality, pif_mask, counts[None])
    for group in groups:
        tile = sum(parts_of(tile, group))
    tile = near(tile + swap(tile, 1))
    got = near(swap(send, top))
    keep, copy = near(keep), near(copy)
    part = pl.pallas_call(
        functools.partial(partial_kernel, size),
        out_shape=pltpu.VMEM(shape[1:], F32),
        in_specs=[VMEM] * 3,
        out_specs=VMEM,
    )(keep, got, tile)
    parts = parts_of(part, [1])
    for group in groups:
        parts = parts_of(sum(parts), group)
    sums = pltpu.VMEM((dates, 4, rows, LANES), F32)
    own, other = pl.pallas_call(
        functools.partial(fit_kernel, size),
        out_shape=[sums, sums],
        in_specs=[VMEM] * (3 + len(parts)),
        out_specs=[VMEM] * 2,
    )(keep, got, tile, *map(near, parts))
    out = pl.pallas_call(
        apply_kernel,
        out_shape=jax.ShapeDtypeStruct(scenes.shape, scenes.dtype),
        in_specs=[VMEM] * 3,
        out_specs=VMEM,
    )(near(own), near(swap(other, top)), copy)
    return out.transpose(0, 2, 1, 3)


def solution(mesh):
    placed = (
        P(("groups", "dates"), None, None, None),
        P(("groups", "dates"), None, None),
        P(("groups", "dates"), None),
        P(("groups", "dates")),
    )
    return jax.shard_map(
        functools.partial(local, mesh.shape["dates"]),
        mesh=mesh,
        in_specs=placed,
        out_specs=P(("groups", "dates"), None, None, None),
        check_vma=False,
    )
```

```python
import functools
import jax
import jax.numpy as jnp
from jax import lax
from jax.experimental import pallas as pl
from jax.experimental.pallas import tpu as pltpu
from jax.sharding import PartitionSpec as P

F32 = jnp.float32
LANES = 128
CORES = 2
VMEM = pl.BlockSpec(memory_space=pltpu.VMEM)
SMEM = pl.BlockSpec(memory_space=pltpu.SMEM)


def near(x):
    return pltpu.with_memory_space_constraint(x, pltpu.VMEM)


def chip_pairs(chips):
    half = chips // 2
    near_by = list(range(3, half + 1)) + [2]
    return list(zip(near_by, range(half + 1, chips))) + [(1, 1)]


def way_back(pairs):
    order = list(range(len(pairs)))
    return order[-2:] + order[:-2][::-1]


def place():
    me = lax.axis_index("dates")
    return me // CORES, me % CORES


def met_chip(pair):
    chip, core = place()
    return chip ^ jnp.where(core == 0, pair[0], pair[1])


def load_kernel(*refs):
    count = len(refs) // 2
    for ref, out in zip(refs[:count], refs[count:]):
        out[...] = ref[...]


def info_kernel(pif_ref, counts_ref, out_ref):
    tiles, width = out_ref.shape
    pixels = pif_ref.shape[-1]
    _, core = place()
    row = lax.broadcasted_iota(jnp.int32, (tiles, width), 0)
    count = jnp.full((tiles, LANES), counts_ref[0], jnp.int32).astype(F32)
    pif = jnp.broadcast_to(pif_ref[...], (tiles, pixels))
    out_ref[...] = jnp.where(row == core, jnp.concatenate([pif, count], axis=1), 0.0)


def pack_kernel(pairs, own_s, own_q, mate_s, mate_q, *out_refs):
    dates, bands, tiles, pixels = own_s.shape
    rows, per = bands + 1, CORES
    _, core = place()
    out_rows = len(out_refs) * rows * per
    row = lax.broadcasted_iota(jnp.int32, (out_rows, rows * tiles), 0)
    column = lax.broadcasted_iota(jnp.int32, (out_rows, rows * tiles), 1)
    slot, rest = row // (rows * per), row % (rows * per)
    target = jnp.zeros_like(row)
    for s, pair in enumerate([(0, 0)] + pairs):
        target = jnp.where(slot == s, met_chip(pair), target)
    wanted = rest // per * tiles + target * per + rest % per
    choose = (column == wanted).astype(own_s.dtype)
    for first, scenes, quality in ((core, own_s, own_q), (1 - core, mate_s, mate_q)):
        for d in range(dates):
            flat = jnp.concatenate(
                [scenes[d].reshape(bands * tiles, pixels), quality[d]], axis=0
            )
            picked = jnp.dot(choose, flat, preferred_element_type=F32)
            for s, out in enumerate(out_refs):
                block = picked[s * rows * per : (s + 1) * rows * per]
                if out.shape[0] > dates:
                    out[first * dates + d] = block.astype(out.dtype)
                elif scenes is own_s:
                    out[d] = block.astype(out.dtype)


def spread(pair_rows, rows):
    shape = (rows,) + pair_rows.shape[1:]
    row = lax.broadcasted_iota(jnp.int32, shape, 0)
    return jnp.where(
        row % CORES == 0,
        jnp.broadcast_to(pair_rows[:1], shape),
        jnp.broadcast_to(pair_rows[1:2], shape),
    )


def dates_of(pairs, refs, counts, dates):
    _, core = place()
    _, rows, pixels = refs[0].shape
    row = lax.broadcasted_iota(jnp.int32, (rows, pixels), 0)
    for s, (ref, pair) in enumerate(zip(refs, [(0, 0)] + pairs)):
        skipped = core * dates if pair[0] == pair[1] else 0
        held = []
        for j in range(ref.shape[0]):
            both = ref[j].astype(F32)
            date = met_chip(pair) * (CORES * dates) + skipped + j
            covered = (counts > date.astype(F32)).astype(F32)
            covered = jnp.concatenate([covered] * (pixels // LANES), axis=1)
            weight = both[rows - CORES :] * covered
            values = jnp.where(row < rows - CORES, both, 1.0)
            held.append((4 * (skipped + j), values, spread(weight, rows)))
        yield s, held


def partial_kernel(pairs, dates, info_ref, *refs):
    *refs, out_ref = refs
    pixels = refs[0].shape[-1]
    total = jnp.zeros(out_ref.shape, F32)
    for _, held in dates_of(pairs, refs, info_ref[:, pixels:], dates):
        for _, values, weight in held:
            total += weight * values
    out_ref[...] = total


def columns_of(terms, rows):
    lane = lax.broadcasted_iota(jnp.int32, (rows, LANES), 1)
    block = jnp.zeros((rows, LANES), F32)
    for k, term in terms:
        total = jnp.sum(term, axis=1, keepdims=True)
        block = jnp.where(lane == k, total, block)
    return block


def own_sums_kernel(pairs, dates, info_ref, *refs):
    count = len(pairs) + 1
    refs, out_refs = refs[:count], refs[count:]
    _, rows, pixels = refs[0].shape
    pif = spread(info_ref[:, :pixels], rows)
    for s, held in dates_of(pairs, refs, info_ref[:, pixels:], dates):
        terms = []
        for k, values, weight in held:
            fitted = weight * pif * values
            terms += [(k, fitted), (k + 1, fitted * values)]
        out_refs[s][...] = columns_of(terms, rows)


def cross_sums_kernel(pairs, dates, info_ref, part_ref, got_ref, *refs):
    count = len(pairs) + 1
    refs, own_refs, out_refs = refs[:count], refs[count : 2 * count], refs[2 * count :]
    _, rows, pixels = refs[0].shape
    pif = spread(info_ref[:, :pixels], rows)
    total = part_ref[...] + got_ref[...]
    composite = total / spread(total[rows - CORES :], rows)
    for s, held in dates_of(pairs, refs, info_ref[:, pixels:], dates):
        terms = []
        for k, values, weight in held:
            fit = weight * pif * composite
            terms += [(k + 2, fit), (k + 3, fit * values)]
        out_refs[s][...] = own_refs[s][...] + columns_of(terms, rows)


def sum_kernel(*refs):
    *refs, out_ref = refs
    out_ref[...] = sum(ref[...] for ref in refs)


def apply_kernel(sums_ref, got_ref, scenes_ref, out_ref):
    dates, bands, tiles, pixels = scenes_ref.shape
    _, core = place()
    sums = sums_ref[...] + got_ref[...]
    sums = jnp.where(core == 0, sums, pltpu.roll(sums, LANES - 4 * dates, 1))
    sum_x = sums + pltpu.roll(sums, sums.shape[0] - 1, 0)
    sum_xx, sum_y, sum_xy = (pltpu.roll(sum_x, LANES - k, 1) for k in (1, 2, 3))
    last = CORES * bands
    total = jnp.broadcast_to(sum_x[last : last + 1], sums.shape)
    mean_x = sum_x / total
    mean_y = sum_y / total
    spread_x = sum_xx / total - mean_x * mean_x + 1e-05
    gain = (sum_xy / total - mean_x * mean_y) / spread_x
    offset = mean_y - gain * mean_x
    for d in range(dates):
        shape = (sums.shape[0], pixels)
        slope, shift = (
            jnp.broadcast_to(x[:, 4 * d : 4 * d + 1], shape) for x in (gain, offset)
        )
        for b in range(bands):
            r = CORES * b
            values = scenes_ref[d, b].astype(F32)
            out_ref[d, b] = (slope[r : r + 1] * values + shift[r : r + 1]).astype(
                out_ref.dtype
            )


def local(size, scenes, quality, pif_mask, counts):
    dates, tiles, bands, pixels = scenes.shape
    scenes = scenes.transpose(0, 2, 1, 3)
    rows = (bands + 1) * CORES
    pairs = chip_pairs(size // CORES)

    def swap(x, near_far):
        hop = [CORES * k for k in near_far]
        return lax.ppermute(x, "dates", [(i, i ^ hop[i % CORES]) for i in range(size)])

    def mate(x):
        return lax.ppermute(x, "dates", [(i, i ^ 1) for i in range(size)])

    arguments = {id(x) for x in (scenes, quality, pif_mask, counts)}

    def call(kernel, out_shape, *args, in_specs=None):
        many = isinstance(out_shape, list)
        args = [x if id(x) in arguments else near(x) for x in args]
        return pl.pallas_call(
            kernel,
            out_shape=out_shape,
            in_specs=in_specs or [VMEM] * len(args),
            out_specs=[VMEM] * len(out_shape) if many else VMEM,
        )(*args)

    mate_scenes, mate_quality = mate(scenes), mate(quality)
    own_scenes, own_quality, own_pif = call(
        load_kernel,
        [pltpu.VMEM(x.shape, x.dtype) for x in (scenes, quality, pif_mask)],
        scenes,
        quality,
        pif_mask,
    )
    blocks = [
        pltpu.VMEM((dates * (1 if a == b else CORES), rows, pixels), scenes.dtype)
        for a, b in [(0, 0)] + pairs
    ]
    own, *sent = call(
        functools.partial(pack_kernel, pairs),
        blocks,
        own_scenes,
        own_quality,
        mate_scenes,
        mate_quality,
    )
    info = call(
        info_kernel,
        pltpu.VMEM((CORES, pixels + LANES), F32),
        own_pif,
        counts,
        in_specs=[VMEM, SMEM],
    )
    info = info + mate(info)
    held = [own] + [swap(x, pair) for x, pair in zip(sent, pairs)]
    part = call(
        functools.partial(partial_kernel, pairs, dates),
        pltpu.VMEM((rows, pixels), F32),
        info,
        *held,
    )
    sums = [pltpu.VMEM((rows, LANES), F32)] * len(held)
    own_sums = call(
        functools.partial(own_sums_kernel, pairs, dates), sums, info, *held
    )
    own, *sent = call(
        functools.partial(cross_sums_kernel, pairs, dates),
        sums,
        info,
        part,
        mate(part),
        *held,
        *own_sums,
    )
    back = [swap(sent[s], pairs[s]) for s in way_back(pairs)]
    total = call(sum_kernel, sums[0], own, *back)
    out = call(
        apply_kernel,
        jax.ShapeDtypeStruct(scenes.shape, scenes.dtype),
        total,
        mate(total),
        own_scenes,
    )
    return out.transpose(0, 2, 1, 3)


def solution(mesh):
    placed = (
        P(("groups", "dates"), None, None, None),
        P(("groups", "dates"), None, None),
        P(("groups", "dates"), None),
        P(("groups", "dates")),
    )
    return jax.shard_map(
        functools.partial(local, mesh.shape["dates"]),
        mesh=mesh,
        in_specs=placed,
        out_specs=P(("groups", "dates"), None, None, None),
        check_vma=False,
    )
```

```python
import functools
import jax
import jax.numpy as jnp
from jax import lax
from jax.experimental import pallas as pl
from jax.experimental.pallas import tpu as pltpu
from jax.sharding import PartitionSpec as P

F32 = jnp.float32
LANES = 128
CORES = 2
VMEM = pl.BlockSpec(memory_space=pltpu.VMEM)
SMEM = pl.BlockSpec(memory_space=pltpu.SMEM)


def near(x):
    return pltpu.with_memory_space_constraint(x, pltpu.VMEM)


def chip_pairs(chips):
    odd = list(range(3, chips, 2))
    return list(zip(range(chips - 2, 0, -2), odd[1:] + odd[:1])) + [(1, 1)]


def way_back(pairs):
    couples = sorted((a, a + 1) for a, b in pairs if a != b)
    first = couples.pop(len(couples) // 2) if couples else (1, 1)
    return [first] + [(1, 1)] * bool(pairs[1:]) + couples


def place():
    me = lax.axis_index("dates")
    return me // CORES, me % CORES


def met_chip(pair):
    chip, core = place()
    return chip ^ jnp.where(core == 0, pair[0], pair[1])


def load_kernel(*refs):
    count = len(refs) // 2
    for ref, out in zip(refs[:count], refs[count:]):
        out[...] = ref[...]


def info_kernel(pif_ref, counts_ref, out_ref):
    tiles, width = out_ref.shape
    pixels = pif_ref.shape[-1]
    _, core = place()
    row = lax.broadcasted_iota(jnp.int32, (tiles, width), 0)
    count = jnp.full((tiles, LANES), counts_ref[0], jnp.int32).astype(F32)
    pif = jnp.broadcast_to(pif_ref[...], (tiles, pixels))
    out_ref[...] = jnp.where(row == core, jnp.concatenate([pif, count], axis=1), 0.0)


def pack_kernel(pairs, own_s, own_q, mate_s, mate_q, *out_refs):
    dates, bands, tiles, pixels = own_s.shape
    rows, per = bands + 1, CORES
    _, core = place()
    out_rows = len(out_refs) * rows * per
    row = lax.broadcasted_iota(jnp.int32, (out_rows, rows * tiles), 0)
    column = lax.broadcasted_iota(jnp.int32, (out_rows, rows * tiles), 1)
    slot, rest = row // (rows * per), row % (rows * per)
    target = jnp.zeros_like(row)
    for s, pair in enumerate([(0, 0)] + pairs):
        target = jnp.where(slot == s, met_chip(pair), target)
    wanted = rest // per * tiles + target * per + rest % per
    choose = (column == wanted).astype(own_s.dtype)
    for first, scenes, quality in ((core, own_s, own_q), (1 - core, mate_s, mate_q)):
        for d in range(dates):
            flat = jnp.concatenate(
                [scenes[d].reshape(bands * tiles, pixels), quality[d]], axis=0
            )
            picked = jnp.dot(choose, flat, preferred_element_type=F32)
            for s, out in enumerate(out_refs):
                block = picked[s * rows * per : (s + 1) * rows * per]
                if out.shape[0] > dates:
                    out[first * dates + d] = block.astype(out.dtype)
                elif scenes is own_s:
                    out[d] = block.astype(out.dtype)


def spread(pair_rows, rows):
    shape = (rows,) + pair_rows.shape[1:]
    row = lax.broadcasted_iota(jnp.int32, shape, 0)
    return jnp.where(
        row % CORES == 0,
        jnp.broadcast_to(pair_rows[:1], shape),
        jnp.broadcast_to(pair_rows[1:2], shape),
    )


def dates_of(pairs, refs, counts, dates):
    _, core = place()
    _, rows, pixels = refs[0].shape
    row = lax.broadcasted_iota(jnp.int32, (rows, pixels), 0)
    for s, (ref, pair) in enumerate(zip(refs, [(0, 0)] + pairs)):
        skipped = core * dates if pair[0] == pair[1] else 0
        held = []
        for j in range(ref.shape[0]):
            both = ref[j].astype(F32)
            date = met_chip(pair) * (CORES * dates) + skipped + j
            covered = (counts > date.astype(F32)).astype(F32)
            covered = jnp.concatenate([covered] * (pixels // LANES), axis=1)
            weight = both[rows - CORES :] * covered
            values = jnp.where(row < rows - CORES, both, 1.0)
            held.append((4 * (skipped + j), values, spread(weight, rows)))
        yield s, held


def partial_kernel(pairs, dates, info_ref, *refs):
    *refs, out_ref = refs
    pixels = refs[0].shape[-1]
    total = jnp.zeros(out_ref.shape, F32)
    for _, held in dates_of(pairs, refs, info_ref[:, pixels:], dates):
        for _, values, weight in held:
            total += weight * values
    out_ref[...] = total


def columns_of(terms, rows):
    lane = lax.broadcasted_iota(jnp.int32, (rows, LANES), 1)
    block = jnp.zeros((rows, LANES), F32)
    for k, term in terms:
        total = jnp.sum(term, axis=1, keepdims=True)
        block = jnp.where(lane == k, total, block)
    return block


def own_sums_kernel(pairs, dates, info_ref, *refs):
    count = len(pairs) + 1
    refs, out_refs = refs[:count], refs[count:]
    _, rows, pixels = refs[0].shape
    pif = spread(info_ref[:, :pixels], rows)
    for s, held in dates_of(pairs, refs, info_ref[:, pixels:], dates):
        terms = []
        for k, values, weight in held:
            fitted = weight * pif * values
            terms += [(k, fitted), (k + 1, fitted * values)]
        out_refs[s][...] = columns_of(terms, rows)


def cross_sums_kernel(pairs, dates, info_ref, part_ref, got_ref, *refs):
    count = len(pairs) + 1
    refs, own_refs, out_refs = refs[:count], refs[count : 2 * count], refs[2 * count :]
    _, rows, pixels = refs[0].shape
    pif = spread(info_ref[:, :pixels], rows)
    total = part_ref[...] + got_ref[...]
    composite = total / spread(total[rows - CORES :], rows)
    blocks = []
    for s, held in dates_of(pairs, refs, info_ref[:, pixels:], dates):
        terms = []
        for k, values, weight in held:
            fit = weight * pif * composite
            terms += [(k + 2, fit), (k + 3, fit * values)]
        blocks.append(own_refs[s][...] + columns_of(terms, rows))
    _, core = place()
    out_refs[0][...] = blocks[0]
    near_by, far_off = zip(*pairs)
    for out, (a, b) in zip(out_refs[1:], way_back(pairs)):
        first, second = near_by.index(a) + 1, far_off.index(b) + 1
        out[...] = jnp.where(core == 0, blocks[first], blocks[second])


def sum_kernel(*refs):
    *refs, out_ref = refs
    out_ref[...] = sum(ref[...] for ref in refs)


def apply_kernel(sums_ref, got_ref, scenes_ref, out_ref, done_ref, sems):
    dates, bands, tiles, pixels = scenes_ref.shape
    _, core = place()
    sums = sums_ref[...] + got_ref[...]
    sum_x = sums + pltpu.roll(sums, sums.shape[0] - 1, 0)
    sum_xx, sum_y, sum_xy = (pltpu.roll(sum_x, LANES - k, 1) for k in (1, 2, 3))
    last = CORES * bands
    total = jnp.broadcast_to(sum_x[last : last + 1], sums.shape)
    mean_x = sum_x / total
    mean_y = sum_y / total
    spread_x = sum_xx / total - mean_x * mean_x + 1e-05
    gain = (sum_xy / total - mean_x * mean_y) / spread_x
    offset = mean_y - gain * mean_x
    copies = []
    for d in range(dates):
        shape = (sums.shape[0], pixels)
        slope, shift = (
            jnp.where(
                core == 0,
                jnp.broadcast_to(x[:, 4 * d : 4 * d + 1], shape),
                jnp.broadcast_to(x[:, 4 * (d + dates) : 4 * (d + dates) + 1], shape),
            )
            for x in (gain, offset)
        )
        for b in range(bands):
            r = CORES * b
            values = scenes_ref[d, b].astype(F32)
            done_ref[d, b] = (slope[r : r + 1] * values + shift[r : r + 1]).astype(
                done_ref.dtype
            )
        copies.append(pltpu.make_async_copy(done_ref.at[d], out_ref.at[d], sems.at[d]))
        copies[-1].start()
    for copy in copies:
        copy.wait()


def local(size, scenes, quality, pif_mask, counts):
    dates, tiles, bands, pixels = scenes.shape
    scenes = scenes.transpose(0, 2, 1, 3)
    rows = (bands + 1) * CORES
    pairs = chip_pairs(size // CORES)

    def swap(x, near_far):
        hop = [CORES * k for k in near_far]
        return lax.ppermute(x, "dates", [(i, i ^ hop[i % CORES]) for i in range(size)])

    def mate(x):
        return lax.ppermute(x, "dates", [(i, i ^ 1) for i in range(size)])

    arguments = {id(x) for x in (scenes, quality, pif_mask, counts)}

    def call(kernel, out_shape, *args, in_specs=None):
        many = isinstance(out_shape, list)
        args = [x if id(x) in arguments else near(x) for x in args]
        return pl.pallas_call(
            kernel,
            out_shape=out_shape,
            in_specs=in_specs or [VMEM] * len(args),
            out_specs=[VMEM] * len(out_shape) if many else VMEM,
        )(*args)

    mate_scenes, mate_quality = mate(scenes), mate(quality)
    own_scenes, own_quality, own_pif = call(
        load_kernel,
        [pltpu.VMEM(x.shape, x.dtype) for x in (scenes, quality, pif_mask)],
        scenes,
        quality,
        pif_mask,
    )
    blocks = [
        pltpu.VMEM((dates * (1 if a == b else CORES), rows, pixels), scenes.dtype)
        for a, b in [(0, 0)] + pairs
    ]
    own, *sent = call(
        functools.partial(pack_kernel, pairs),
        blocks,
        own_scenes,
        own_quality,
        mate_scenes,
        mate_quality,
    )
    info = call(
        info_kernel,
        pltpu.VMEM((CORES, pixels + LANES), F32),
        own_pif,
        counts,
        in_specs=[VMEM, SMEM],
    )
    info = info + mate(info)
    held = [own] + [swap(x, pair) for x, pair in zip(sent, pairs)]
    part = call(
        functools.partial(partial_kernel, pairs, dates),
        pltpu.VMEM((rows, pixels), F32),
        info,
        *held,
    )
    sums = [pltpu.VMEM((rows, LANES), F32)] * len(held)
    own_sums = call(
        functools.partial(own_sums_kernel, pairs, dates), sums, info, *held
    )
    own, *sent = call(
        functools.partial(cross_sums_kernel, pairs, dates),
        sums,
        info,
        part,
        mate(part),
        *held,
        *own_sums,
    )
    back = [swap(x, pair) for x, pair in zip(sent, way_back(pairs))]
    total = call(sum_kernel, sums[0], own, *back)
    out = pl.pallas_call(
        apply_kernel,
        out_shape=jax.ShapeDtypeStruct(scenes.shape, scenes.dtype),
        in_specs=[VMEM] * 3,
        out_specs=pl.BlockSpec(memory_space=pl.ANY),
        scratch_shapes=[
            pltpu.VMEM(scenes.shape, scenes.dtype),
            pltpu.SemaphoreType.DMA((dates,)),
        ],
    )(near(total), near(mate(total)), near(own_scenes))
    return out.transpose(0, 2, 1, 3)


def solution(mesh):
    placed = (
        P(("groups", "dates"), None, None, None),
        P(("groups", "dates"), None, None),
        P(("groups", "dates"), None),
        P(("groups", "dates")),
    )
    return jax.shard_map(
        functools.partial(local, mesh.shape["dates"]),
        mesh=mesh,
        in_specs=placed,
        out_specs=P(("groups", "dates"), None, None, None),
        check_vma=False,
    )
```

```python
import functools
import jax
import jax.numpy as jnp
from jax import lax
from jax.experimental import pallas as pl
from jax.experimental.pallas import tpu as pltpu
from jax.sharding import PartitionSpec as P

F32 = jnp.float32
LANES = 128
CORES = 2
VMEM = pl.BlockSpec(memory_space=pltpu.VMEM)
SMEM = pl.BlockSpec(memory_space=pltpu.SMEM)


def near(x):
    return pltpu.with_memory_space_constraint(x, pltpu.VMEM)


NEXT = (1, 1)


def chip_pairs(chips):
    odd = list(range(3, chips, 2))
    return list(zip(range(chips - 2, 0, -2), odd[1:] + odd[:1]))


def way_back(pairs):
    couples = sorted((a, a + 1) for a, b in pairs)
    first = couples.pop(len(couples) // 2)
    return [first] + couples


def place():
    me = lax.axis_index("dates")
    return me // CORES, me % CORES


def met_chip(pair):
    chip, core = place()
    return chip ^ jnp.where(core == 0, pair[0], pair[1])


def load_kernel(*refs):
    count = len(refs) // 2
    for ref, out in zip(refs[:count], refs[count:]):
        out[...] = ref[...]


def info_kernel(pif_ref, counts_ref, out_ref):
    tiles, width = out_ref.shape
    pixels = pif_ref.shape[-1]
    _, core = place()
    row = lax.broadcasted_iota(jnp.int32, (tiles, width), 0)
    count = jnp.full((tiles, LANES), counts_ref[0], jnp.int32).astype(F32)
    pif = jnp.broadcast_to(pif_ref[...], (tiles, pixels))
    out_ref[...] = jnp.where(row == core, jnp.concatenate([pif, count], axis=1), 0.0)


def pack_kernel(pairs, own_s, own_q, mate_s, mate_q, *out_refs):
    dates, bands, tiles, pixels = own_s.shape
    rows, per = bands + 1, CORES
    _, core = place()
    out_rows = len(out_refs) * rows * per
    row = lax.broadcasted_iota(jnp.int32, (out_rows, rows * tiles), 0)
    column = lax.broadcasted_iota(jnp.int32, (out_rows, rows * tiles), 1)
    slot, rest = row // (rows * per), row % (rows * per)
    target = jnp.zeros_like(row)
    for s, pair in enumerate([(0, 0), NEXT] + pairs):
        target = jnp.where(slot == s, met_chip(pair), target)
    wanted = rest // per * tiles + target * per + rest % per
    choose = (column == wanted).astype(own_s.dtype)
    for first, scenes, quality in ((core, own_s, own_q), (1 - core, mate_s, mate_q)):
        for d in range(dates):
            flat = jnp.concatenate(
                [scenes[d].reshape(bands * tiles, pixels), quality[d]], axis=0
            )
            picked = jnp.dot(choose, flat, preferred_element_type=F32)
            for s, out in enumerate(out_refs):
                block = picked[s * rows * per : (s + 1) * rows * per]
                out[first * dates + d] = block.astype(out.dtype)


def spread(pair_rows, rows):
    shape = (rows,) + pair_rows.shape[1:]
    row = lax.broadcasted_iota(jnp.int32, shape, 0)
    return jnp.where(
        row % CORES == 0,
        jnp.broadcast_to(pair_rows[:1], shape),
        jnp.broadcast_to(pair_rows[1:2], shape),
    )


def dates_of(ref, pair, counts, dates, mine=False):
    _, core = place()
    held, rows, pixels = ref.shape
    row = lax.broadcasted_iota(jnp.int32, (rows, pixels), 0)
    for j in range(dates if mine else held):
        at = core * dates + j if mine else j
        both = ref[at].astype(F32)
        date = met_chip(pair) * held + at
        covered = (counts > date.astype(F32)).astype(F32)
        covered = jnp.concatenate([covered] * (pixels // LANES), axis=1)
        weight = both[rows - CORES :] * covered
        values = jnp.where(row < rows - CORES, both, 1.0)
        yield 4 * j, values, spread(weight, rows)


def weighted(refs, pairs, counts, dates):
    return sum(
        weight * values
        for ref, pair in zip(refs, pairs)
        for _, values, weight in dates_of(ref, pair, counts, dates)
    )


def partial_kernel(pairs, dates, info_ref, *refs):
    *refs, out_ref = refs
    counts = info_ref[:, refs[0].shape[-1] :]
    out_ref[...] = weighted(refs, pairs, counts, dates)


def columns_of(terms, rows):
    lane = lax.broadcasted_iota(jnp.int32, (rows, LANES), 1)
    block = jnp.zeros((rows, LANES), F32)
    for k, term in terms:
        total = jnp.sum(term, axis=1, keepdims=True)
        block = jnp.where(lane == k, total, block)
    return block


def own_sums_kernel(pairs, dates, info_ref, own_ref, *refs):
    count = len(pairs)
    refs, part_ref, out_refs = refs[:count], refs[count], refs[count + 1 :]
    _, rows, pixels = own_ref.shape
    counts = info_ref[:, pixels:]
    pif = spread(info_ref[:, :pixels], rows)
    part_ref[...] = weighted([own_ref], [(0, 0)], counts, dates)
    blocks = [(own_ref, (0, 0), True)] + [(r, p, False) for r, p in zip(refs, pairs)]
    for out, (ref, pair, mine) in zip(out_refs, blocks):
        terms = []
        for k, values, weight in dates_of(ref, pair, counts, dates, mine):
            fitted = weight * pif * values
            terms += [(k, fitted), (k + 1, fitted * values)]
        out[...] = columns_of(terms, rows)


def cross_sums_kernel(pairs, dates, info_ref, next_ref, own_ref, *refs):
    count = len(pairs)
    refs, (mine_ref, mate_ref, here_ref, own_sums, *sums), out_refs = (
        refs[:count],
        refs[count : 2 * count + 4],
        refs[2 * count + 4 :],
    )
    _, rows, pixels = own_ref.shape
    counts = info_ref[:, pixels:]
    pif = spread(info_ref[:, :pixels], rows)
    total = mine_ref[...] + mate_ref[...] + here_ref[...]
    total += weighted([next_ref], [NEXT], counts, dates)
    composite = total / spread(total[rows - CORES :], rows)

    def block(ref, pair, mine, add):
        terms = []
        for k, values, weight in dates_of(ref, pair, counts, dates, mine):
            fit = weight * pif * composite
            terms += [(k + 2, fit), (k + 3, fit * values)]
        return columns_of(terms, rows) + add[...]

    for k, values, weight in dates_of(next_ref, NEXT, counts, dates, True):
        fit = weight * pif
        cross = fit * composite
        terms = (fit * values, fit * values * values, cross, cross * values)
        terms = [(k + extra, term) for extra, term in enumerate(terms)]
        out_refs[1][k // 4] = columns_of(terms, rows)
    out_refs[0][...] = block(own_ref, (0, 0), True, own_sums)
    blocks = [block(r, p, False, add) for r, p, add in zip(refs, pairs, sums)]
    _, core = place()
    near_by, far_off = zip(*pairs)
    for out, (a, b) in zip(out_refs[2:], way_back(pairs)):
        out[...] = jnp.where(
            core == 0, blocks[near_by.index(a)], blocks[far_off.index(b)]
        )


def sum_kernel(*refs):
    *refs, out_ref = refs
    out_ref[...] = sum(ref[...] for ref in refs)


def join_kernel(dates, own_ref, mine_ref, mate_ref, out_ref):
    _, core = place()
    sums = mine_ref[...] + mate_ref[...]
    sums = jnp.where(core == 0, sums, pltpu.roll(sums, LANES - 4 * dates, 1))
    out_ref[...] = own_ref[...] + sums


def apply_kernel(sums_ref, got_ref, scenes_ref, out_ref, done_ref, sems):
    dates, bands, tiles, pixels = scenes_ref.shape
    sums = sums_ref[...] + jnp.sum(got_ref[...], axis=0)
    sum_x = sums + pltpu.roll(sums, sums.shape[0] - 1, 0)
    sum_xx, sum_y, sum_xy = (pltpu.roll(sum_x, LANES - k, 1) for k in (1, 2, 3))
    last = CORES * bands
    total = jnp.broadcast_to(sum_x[last : last + 1], sums.shape)
    mean_x = sum_x / total
    mean_y = sum_y / total
    spread_x = sum_xx / total - mean_x * mean_x + 1e-05
    gain = (sum_xy / total - mean_x * mean_y) / spread_x
    offset = mean_y - gain * mean_x
    copies = []
    for d in range(dates):
        shape = (sums.shape[0], pixels)
        slope, shift = (
            jnp.broadcast_to(x[:, 4 * d : 4 * d + 1], shape) for x in (gain, offset)
        )
        for b in range(bands):
            r = CORES * b
            values = scenes_ref[d, b].astype(F32)
            done_ref[d, b] = (slope[r : r + 1] * values + shift[r : r + 1]).astype(
                done_ref.dtype
            )
        copies.append(pltpu.make_async_copy(done_ref.at[d], out_ref.at[d], sems.at[d]))
        copies[-1].start()
    for copy in copies:
        copy.wait()


def local(size, scenes, quality, pif_mask, counts):
    dates, tiles, bands, pixels = scenes.shape
    scenes = scenes.transpose(0, 2, 1, 3)
    rows = (bands + 1) * CORES
    pairs = chip_pairs(size // CORES)

    def swap(x, near_far):
        hop = [CORES * k for k in near_far]
        return lax.ppermute(x, "dates", [(i, i ^ hop[i % CORES]) for i in range(size)])

    def mate(x):
        return lax.ppermute(x, "dates", [(i, i ^ 1) for i in range(size)])

    arguments = {id(x) for x in (scenes, quality, pif_mask, counts)}

    def call(kernel, out_shape, *args, in_specs=None):
        many = isinstance(out_shape, list)
        args = [x if id(x) in arguments else near(x) for x in args]
        return pl.pallas_call(
            kernel,
            out_shape=out_shape,
            in_specs=in_specs or [VMEM] * len(args),
            out_specs=[VMEM] * len(out_shape) if many else VMEM,
        )(*args)

    mate_scenes, mate_quality = mate(scenes), mate(quality)
    own_scenes, own_quality, own_pif = call(
        load_kernel,
        [pltpu.VMEM(x.shape, x.dtype) for x in (scenes, quality, pif_mask)],
        scenes,
        quality,
        pif_mask,
    )
    block = pltpu.VMEM((CORES * dates, rows, pixels), scenes.dtype)
    own, beside, *sent = call(
        functools.partial(pack_kernel, pairs),
        [block] * (len(pairs) + 2),
        own_scenes,
        own_quality,
        mate_scenes,
        mate_quality,
    )
    info = call(
        info_kernel,
        pltpu.VMEM((CORES, pixels + LANES), F32),
        own_pif,
        counts,
        in_specs=[VMEM, SMEM],
    )
    info = info + mate(info)
    held = [swap(x, pair) for x, pair in zip(sent, pairs)]
    beside = swap(beside, NEXT)
    wide = pltpu.VMEM((rows, pixels), F32)
    sums = pltpu.VMEM((rows, LANES), F32)
    part = call(functools.partial(partial_kernel, pairs, dates), wide, info, *held)
    here, *own_sums = call(
        functools.partial(own_sums_kernel, pairs, dates),
        [wide] + [sums] * (len(pairs) + 1),
        info,
        own,
        *held,
    )
    own, beside, *sent = call(
        functools.partial(cross_sums_kernel, pairs, dates),
        [sums, pltpu.VMEM((dates, rows, LANES), F32)] + [sums] * len(pairs),
        info,
        beside,
        own,
        *held,
        part,
        mate(part),
        here,
        *own_sums,
    )
    back = [swap(x, pair) for x, pair in zip(sent, way_back(pairs))]
    beside = swap(beside, NEXT)
    back = call(sum_kernel, sums, *back)
    total = call(
        functools.partial(join_kernel, dates), sums, own, back, mate(back)
    )
    out = pl.pallas_call(
        apply_kernel,
        out_shape=jax.ShapeDtypeStruct(scenes.shape, scenes.dtype),
        in_specs=[VMEM] * 3,
        out_specs=pl.BlockSpec(memory_space=pl.ANY),
        scratch_shapes=[
            pltpu.VMEM(scenes.shape, scenes.dtype),
            pltpu.SemaphoreType.DMA((dates,)),
        ],
    )(near(total), near(beside), near(own_scenes))
    return out.transpose(0, 2, 1, 3)


def solution(mesh):
    placed = (
        P(("groups", "dates"), None, None, None),
        P(("groups", "dates"), None, None),
        P(("groups", "dates"), None),
        P(("groups", "dates")),
    )
    return jax.shard_map(
        functools.partial(local, mesh.shape["dates"]),
        mesh=mesh,
        in_specs=placed,
        out_specs=P(("groups", "dates"), None, None, None),
        check_vma=False,
    )
```

```python
import functools
import jax
import jax.numpy as jnp
from jax import lax
from jax.experimental import pallas as pl
from jax.experimental.pallas import tpu as pltpu
from jax.sharding import PartitionSpec as P

F32 = jnp.float32
LANES = 128
CORES = 2
VMEM = pl.BlockSpec(memory_space=pltpu.VMEM)
SMEM = pl.BlockSpec(memory_space=pltpu.SMEM)


def near(x):
    return pltpu.with_memory_space_constraint(x, pltpu.VMEM)


NEXT = (1, 1)


def chip_pairs(chips):
    odd = list(range(3, chips, 2))
    return list(zip(range(chips - 2, 0, -2), odd[1:] + odd[:1]))


def way_back(pairs):
    return sorted(((a, a + 1) for a, b in pairs), reverse=True)


def place():
    me = lax.axis_index("dates")
    return me // CORES, me % CORES


def met_chip(pair):
    chip, core = place()
    return chip ^ jnp.where(core == 0, pair[0], pair[1])


def load_kernel(*refs):
    count = len(refs) // 2
    for ref, out in zip(refs[:count], refs[count:]):
        out[...] = ref[...]


def info_kernel(pif_ref, counts_ref, out_ref):
    tiles, width = out_ref.shape
    pixels = pif_ref.shape[-1]
    _, core = place()
    row = lax.broadcasted_iota(jnp.int32, (tiles, width), 0)
    count = jnp.full((tiles, LANES), counts_ref[0], jnp.int32).astype(F32)
    pif = jnp.broadcast_to(pif_ref[...], (tiles, pixels))
    out_ref[...] = jnp.where(row == core, jnp.concatenate([pif, count], axis=1), 0.0)


def pack_kernel(pairs, own_s, own_q, mate_s, mate_q, *out_refs):
    dates, bands, tiles, pixels = own_s.shape
    rows, per = bands + 1, CORES
    _, core = place()
    out_rows = len(out_refs) * rows * per
    row = lax.broadcasted_iota(jnp.int32, (out_rows, rows * tiles), 0)
    column = lax.broadcasted_iota(jnp.int32, (out_rows, rows * tiles), 1)
    slot, rest = row // (rows * per), row % (rows * per)
    target = jnp.zeros_like(row)
    for s, pair in enumerate([(0, 0), NEXT] + pairs):
        target = jnp.where(slot == s, met_chip(pair), target)
    wanted = rest // per * tiles + target * per + rest % per
    choose = (column == wanted).astype(own_s.dtype)
    for first, scenes, quality in ((core, own_s, own_q), (1 - core, mate_s, mate_q)):
        for d in range(dates):
            flat = jnp.concatenate(
                [scenes[d].reshape(bands * tiles, pixels), quality[d]], axis=0
            )
            picked = jnp.dot(choose, flat, preferred_element_type=F32)
            for s, out in enumerate(out_refs):
                block = picked[s * rows * per : (s + 1) * rows * per]
                out[first * dates + d] = block.astype(out.dtype)


def spread(pair_rows, rows):
    shape = (rows,) + pair_rows.shape[1:]
    row = lax.broadcasted_iota(jnp.int32, shape, 0)
    return jnp.where(
        row % CORES == 0,
        jnp.broadcast_to(pair_rows[:1], shape),
        jnp.broadcast_to(pair_rows[1:2], shape),
    )


def dates_of(ref, pair, counts, dates, mine=False):
    _, core = place()
    held, rows, pixels = ref.shape
    row = lax.broadcasted_iota(jnp.int32, (rows, pixels), 0)
    for j in range(dates if mine else held):
        at = core * dates + j if mine else j
        both = ref[at].astype(F32)
        date = met_chip(pair) * held + at
        covered = (counts > date.astype(F32)).astype(F32)
        covered = jnp.concatenate([covered] * (pixels // LANES), axis=1)
        weight = both[rows - CORES :] * covered
        values = jnp.where(row < rows - CORES, both, 1.0)
        yield 4 * j, values, spread(weight, rows)


def weighted(refs, pairs, counts, dates):
    return sum(
        weight * values
        for ref, pair in zip(refs, pairs)
        for _, values, weight in dates_of(ref, pair, counts, dates)
    )


def partial_kernel(pairs, dates, info_ref, *refs):
    *refs, out_ref = refs
    counts = info_ref[:, refs[0].shape[-1] :]
    out_ref[...] = weighted(refs, pairs, counts, dates)


def columns_of(terms, rows):
    lane = lax.broadcasted_iota(jnp.int32, (rows, LANES), 1)
    block = jnp.zeros((rows, LANES), F32)
    for k, term in terms:
        total = jnp.sum(term, axis=1, keepdims=True)
        block = jnp.where(lane == k, total, block)
    return block


def own_sums_kernel(pairs, dates, info_ref, next_ref, own_ref, *refs):
    count = len(pairs)
    refs, part_ref, out_refs = refs[:count], refs[count], refs[count + 1 :]
    _, rows, pixels = own_ref.shape
    counts = info_ref[:, pixels:]
    pif = spread(info_ref[:, :pixels], rows)
    part_ref[...] = weighted([own_ref, next_ref], [(0, 0), NEXT], counts, dates)
    *out_refs, next_out = out_refs
    for k, values, weight in dates_of(next_ref, NEXT, counts, dates, True):
        fitted = weight * pif * values
        terms = [(k, fitted), (k + 1, fitted * values)]
        next_out[k // 4] = columns_of(terms, rows)
    blocks = [(own_ref, (0, 0), True)] + [(r, p, False) for r, p in zip(refs, pairs)]
    for out, (ref, pair, mine) in zip(out_refs, blocks):
        terms = []
        for k, values, weight in dates_of(ref, pair, counts, dates, mine):
            fitted = weight * pif * values
            terms += [(k, fitted), (k + 1, fitted * values)]
        out[...] = columns_of(terms, rows)


def cross_sums_kernel(pairs, dates, info_ref, next_ref, own_ref, *refs):
    count = len(pairs)
    refs, (mine_ref, mate_ref, here_ref, own_sums, *sums, next_sums), out_refs = (
        refs[:count],
        refs[count : 2 * count + 5],
        refs[2 * count + 5 :],
    )
    _, rows, pixels = own_ref.shape
    counts = info_ref[:, pixels:]
    pif = spread(info_ref[:, :pixels], rows)
    total = mine_ref[...] + mate_ref[...] + here_ref[...]
    composite = total / spread(total[rows - CORES :], rows)

    def block(ref, pair, mine, add):
        terms = []
        for k, values, weight in dates_of(ref, pair, counts, dates, mine):
            fit = weight * pif * composite
            terms += [(k + 2, fit), (k + 3, fit * values)]
        return columns_of(terms, rows) + add[...]

    for k, values, weight in dates_of(next_ref, NEXT, counts, dates, True):
        fit = weight * pif * composite
        terms = [(k + 2, fit), (k + 3, fit * values)]
        out_refs[1][k // 4] = next_sums[k // 4] + columns_of(terms, rows)
    out_refs[0][...] = block(own_ref, (0, 0), True, own_sums)
    blocks = [block(r, p, False, add) for r, p, add in zip(refs, pairs, sums)]
    _, core = place()
    near_by, far_off = zip(*pairs)
    for out, (a, b) in zip(out_refs[2:], way_back(pairs)):
        out[...] = jnp.where(
            core == 0, blocks[near_by.index(a)], blocks[far_off.index(b)]
        )


def sum_kernel(*refs):
    *refs, out_ref = refs
    out_ref[...] = sum(ref[...] for ref in refs)


def join_kernel(dates, own_ref, mine_ref, mate_ref, out_ref):
    _, core = place()
    sums = mine_ref[...] + mate_ref[...]
    sums = jnp.where(core == 0, sums, pltpu.roll(sums, LANES - 4 * dates, 1))
    out_ref[...] = own_ref[...] + sums


def apply_kernel(sums_ref, got_ref, scenes_ref, out_ref, done_ref, sems):
    dates, bands, tiles, pixels = scenes_ref.shape
    sums = sums_ref[...] + jnp.sum(got_ref[...], axis=0)
    sum_x = sums + pltpu.roll(sums, sums.shape[0] - 1, 0)
    sum_xx, sum_y, sum_xy = (pltpu.roll(sum_x, LANES - k, 1) for k in (1, 2, 3))
    last = CORES * bands
    total = jnp.broadcast_to(sum_x[last : last + 1], sums.shape)
    mean_x = sum_x / total
    mean_y = sum_y / total
    spread_x = sum_xx / total - mean_x * mean_x + 1e-05
    gain = (sum_xy / total - mean_x * mean_y) / spread_x
    offset = mean_y - gain * mean_x
    copies = []
    for d in range(dates):
        shape = (sums.shape[0], pixels)
        slope, shift = (
            jnp.broadcast_to(x[:, 4 * d : 4 * d + 1], shape) for x in (gain, offset)
        )
        for b in range(bands):
            r = CORES * b
            values = scenes_ref[d, b].astype(F32)
            done_ref[d, b] = (slope[r : r + 1] * values + shift[r : r + 1]).astype(
                done_ref.dtype
            )
        copies.append(pltpu.make_async_copy(done_ref.at[d], out_ref.at[d], sems.at[d]))
        copies[-1].start()
    for copy in copies:
        copy.wait()


def local(size, scenes, quality, pif_mask, counts):
    dates, tiles, bands, pixels = scenes.shape
    scenes = scenes.transpose(0, 2, 1, 3)
    rows = (bands + 1) * CORES
    pairs = chip_pairs(size // CORES)

    def swap(x, near_far):
        hop = [CORES * k for k in near_far]
        return lax.ppermute(x, "dates", [(i, i ^ hop[i % CORES]) for i in range(size)])

    def mate(x):
        return lax.ppermute(x, "dates", [(i, i ^ 1) for i in range(size)])

    arguments = {id(x) for x in (scenes, quality, pif_mask, counts)}

    def call(kernel, out_shape, *args, in_specs=None):
        many = isinstance(out_shape, list)
        args = [x if id(x) in arguments else near(x) for x in args]
        return pl.pallas_call(
            kernel,
            out_shape=out_shape,
            in_specs=in_specs or [VMEM] * len(args),
            out_specs=[VMEM] * len(out_shape) if many else VMEM,
        )(*args)

    mate_scenes, mate_quality = mate(scenes), mate(quality)
    own_scenes, own_quality, own_pif = call(
        load_kernel,
        [pltpu.VMEM(x.shape, x.dtype) for x in (scenes, quality, pif_mask)],
        scenes,
        quality,
        pif_mask,
    )
    block = pltpu.VMEM((CORES * dates, rows, pixels), scenes.dtype)
    own, beside, *sent = call(
        functools.partial(pack_kernel, pairs),
        [block] * (len(pairs) + 2),
        own_scenes,
        own_quality,
        mate_scenes,
        mate_quality,
    )
    info = call(
        info_kernel,
        pltpu.VMEM((CORES, pixels + LANES), F32),
        own_pif,
        counts,
        in_specs=[VMEM, SMEM],
    )
    info = info + mate(info)
    held = [swap(x, pair) for x, pair in zip(sent, pairs)]
    beside = swap(beside, NEXT)
    wide = pltpu.VMEM((rows, pixels), F32)
    sums = pltpu.VMEM((rows, LANES), F32)
    part = call(functools.partial(partial_kernel, pairs, dates), wide, info, *held)
    here, *own_sums = call(
        functools.partial(own_sums_kernel, pairs, dates),
        [wide] + [sums] * (len(pairs) + 1) + [pltpu.VMEM((dates, rows, LANES), F32)],
        info,
        beside,
        own,
        *held,
    )
    own, beside, *sent = call(
        functools.partial(cross_sums_kernel, pairs, dates),
        [sums, pltpu.VMEM((dates, rows, LANES), F32)] + [sums] * len(pairs),
        info,
        beside,
        own,
        *held,
        part,
        mate(part),
        here,
        *own_sums,
    )
    back = [swap(x, pair) for x, pair in zip(sent, way_back(pairs))]
    beside = swap(beside, NEXT)
    back = call(sum_kernel, sums, *back)
    total = call(
        functools.partial(join_kernel, dates), sums, own, back, mate(back)
    )
    out = pl.pallas_call(
        apply_kernel,
        out_shape=jax.ShapeDtypeStruct(scenes.shape, scenes.dtype),
        in_specs=[VMEM] * 3,
        out_specs=pl.BlockSpec(memory_space=pl.ANY),
        scratch_shapes=[
            pltpu.VMEM(scenes.shape, scenes.dtype),
            pltpu.SemaphoreType.DMA((dates,)),
        ],
    )(near(total), near(beside), near(own_scenes))
    return out.transpose(0, 2, 1, 3)


def solution(mesh):
    placed = (
        P(("groups", "dates"), None, None, None),
        P(("groups", "dates"), None, None),
        P(("groups", "dates"), None),
        P(("groups", "dates")),
    )
    return jax.shard_map(
        functools.partial(local, mesh.shape["dates"]),
        mesh=mesh,
        in_specs=placed,
        out_specs=P(("groups", "dates"), None, None, None),
        check_vma=False,
    )
```
